512 devices in a mesh: chan: 32 (over y, z_hi, core), freq: 16 (over z_lo, x).
Axes of the slice: x: 4, y: 4, z: 16 (z_hi: 4, z_lo: 4; z = z_hi * 4 + z_lo), core: 2. Of those that a mesh axis runs over, the one named last changes fastest.
Arguments:
- traces: bfloat16 [139264, 4096], P('freq', 'chan'), may hold values from -6 to 6
- kept_bins: int32 [128], replicated, may hold values from 1 to 511, as said below
- window_starts: int32 [256], P('freq'), may hold values from 0 to 7680, as said below
Outputs:
- stacked: bfloat16 [4, 2, 128, 4096, 128], P(None, None, 'freq', 'chan')
The draws below stay inside these ranges and needn't reach their ends.
Inputs may be any that keep to these rules, and one draw needn't show every extreme that they name: `kept_bins`: the 128 numbers are distinct; 1 and 511 are always among them. `window_starts`: in each time block of 16 windows the first window starts at 0 and the last at 7680.
All inputs are finite; a program needn't handle non-finite values.
Results may differ from the reference program's by a relative error of at most 0.0064.
Values may be sent and summed in bfloat16 or wider, within the bound.
No kernel may reach another device: no remote copies, remote signals or barrier semaphores. Data moves between devices by JAX's collectives and lax.ppermute only.
A program may use at most 64 MiB of HBM per device.

```python
import math
import jax
import jax.numpy as jnp
from jax import lax

CB = 128
L = 1024
K = 128
ROUNDS = 4
WD = 16
SEG = 8704
CH = 4096
W = 256
S = 139264
N_CHAN = 32


def draw_kept_bins(key, part):
    key = jax.random.fold_in(key, 11)
    first_key, second_key = jax.random.split(key)
    pool = jax.random.permutation(first_key, jnp.arange(2, L // 2 - 1, dtype=jnp.int32))[:K - 2]
    chosen = jnp.concatenate([jnp.array([1, L // 2 - 1], dtype=jnp.int32), pool])
    return jax.random.permutation(second_key, chosen)


def draw_window_starts(key, part):
    key = jax.random.fold_in(key, 23)
    values = jax.random.randint(key, (W // WD, WD), 0, SEG - L + 1, dtype=jnp.int32)
    values = values.at[:, 0].set(0).at[:, WD - 1].set(SEG - L)
    return values.reshape(W)


def levels(key, extent, cuts, least, largest):
    def one(dim, blocks):
        heights = jax.random.uniform(jax.random.fold_in(jax.random.fold_in(key, 6), dim), (blocks,), jnp.float32, least / len(cuts), largest / len(cuts))
        return jnp.repeat(jnp.exp(heights), extent[dim] // blocks).reshape((-1,) + (1,) * (len(extent) - dim - 1))

    level = one(*cuts[0])
    for cut in cuts[1:]:
        level = level * one(*cut)
    return level


def scatter_about(stream_key, shape, spread, bound, pieces=(), held_as=jnp.bfloat16):
    drawn = jax.random.normal(stream_key, shape, jnp.float32) * spread
    if len(pieces) > 0:
        drawn = levels(stream_key, shape, pieces, -0.22, 0.18) * drawn
    return jnp.clip(drawn, min=-bound, max=bound).astype(held_as)


def setup_inputs(seed: int = 0) -> dict:
    splits = jax.random.split(jax.random.key(seed), 4)
    traces = scatter_about(splits[0], (S, CH), 1.0, 6.0, ((0, 16), (1, 32)))
    kept_bins = draw_kept_bins(jax.random.fold_in(splits[3], 71), 0)
    window_starts = draw_window_starts(jax.random.fold_in(splits[3], 71), 0)
    return dict(traces=traces, kept_bins=kept_bins, window_starts=window_starts)


def dft_rows(kept_bins, length):
    sample = jnp.arange(length, dtype=jnp.int32)
    phase = kept_bins[:, None] * sample[None, :] % length
    angle = phase.astype(jnp.float32) * (2.0 * math.pi / length)
    rows = jnp.stack([jnp.cos(angle), -jnp.sin(angle)], axis=1)
    return rows.reshape(2 * kept_bins.shape[0], length).astype(jnp.bfloat16)

def hann_taper(length):
    sample = jnp.arange(length, dtype=jnp.float32)
    return 0.5 - 0.5 * jnp.cos(sample * (2.0 * math.pi / length))

def spectra_of(windows, dft_table):
    values = windows.astype(jnp.float32)
    values = values - lax.optimization_barrier(jnp.mean(values, axis=1, keepdims=True))
    tapered = (values * hann_taper(windows.shape[1])[None, :, None]).astype(jnp.bfloat16)
    spectra = jnp.einsum('jn,wnc->jwc', dft_table.astype(jnp.float32), tapered.astype(jnp.float32))
    spectra = spectra.reshape(dft_table.shape[0] // 2, 2, windows.shape[0], windows.shape[2])
    power = lax.optimization_barrier(jnp.mean(spectra * spectra, axis=(0, 1)))
    return (spectra * lax.rsqrt(power + 1e-06)).astype(jnp.bfloat16)

def cross_spectra(own_spec, far_spec):
    prods = jnp.einsum('kcwa,kdwb->cdkab', own_spec.astype(jnp.float32), far_spec.astype(jnp.float32))
    real_part = prods[0, 0] + prods[1, 1]
    imag_part = prods[1, 0] - prods[0, 1]
    scale = 1.0 / math.sqrt(own_spec.shape[2])
    return (jnp.stack([real_part, imag_part]) * scale).astype(jnp.bfloat16)

def reference(traces, kept_bins, window_starts):
    dft_table = dft_rows(kept_bins, L)
    window_number = jnp.arange(W, dtype=jnp.int32)
    first_sample = window_number // WD * SEG + window_starts
    sample_index = first_sample[:, None] + jnp.arange(L, dtype=jnp.int32)[None, :]

    def block_spectra(block):
        columns = lax.dynamic_slice_in_dim(traces, (block * CB).astype(jnp.int32), CB, 1)
        return spectra_of(columns[sample_index], dft_table)
    blocks = jnp.arange(N_CHAN, dtype=jnp.int32)
    spectra = lax.map(block_spectra, blocks)
    rounds_out = []
    for round_number in range(ROUNDS):

        def pair_block(block, mask_value=round_number + 1):
            partner = jnp.bitwise_xor(block, mask_value).astype(jnp.int32)
            return cross_spectra(spectra[block], spectra[partner])
        result = lax.map(pair_block, blocks)
        rounds_out.append(jnp.transpose(result, (1, 2, 0, 3, 4)).reshape(2, K, CH, CB))
    return jnp.stack(rounds_out)
```

```python
import math

import jax
import jax.numpy as jnp
from jax import lax
from jax.experimental import pallas as pl
from jax.experimental.pallas import tpu as pltpu
from jax.sharding import PartitionSpec as P

L = 1024
K = 128
WD = 16
SEG = 8704
CB = 128
NF = 16
KL = K // NF
HB = KL // 2
SCALE = 1.0 / math.sqrt(NF * WD)
MIB = 1 << 20

SIN_TERMS = [(-1) ** i * (2.0 * math.pi) ** (2 * i + 1) / math.factorial(2 * i + 1) for i in range(7)]


def table_rows(bins):
    shape = (2 * K, L)
    sample = lax.broadcasted_iota(jnp.int32, shape, 1)
    part = lax.broadcasted_iota(jnp.int32, shape, 0) & 1
    phase = (bins * sample + part * (L // 4)) & (L - 1)
    folded = jnp.minimum(phase, L - phase) - L // 4
    turn = folded.astype(jnp.float32) * (1.0 / L)
    square = turn * turn
    total = jnp.full(shape, SIN_TERMS[-1], jnp.float32)
    for term in SIN_TERMS[-2::-1]:
        total = total * square + term
    return (-(total * turn)).astype(jnp.bfloat16)


def front_kernel(starts, half, bins, taper, traces, near, other, wide, table, tapered, spectra):
    table[...] = table_rows(bins[...])
    wide[...] = traces[...].astype(jnp.float32)
    for pair in range(WD // 2):
        slot = tapered.at[pair % 2]
        for side in range(2):
            first = starts[2 * pair + side]
            mean = jnp.sum(wide[pl.ds(first, L), :], axis=0, keepdims=True) * (1.0 / L)
            slot[:, side * CB : (side + 1) * CB] = ((wide[pl.ds(first, L), :] - mean) * taper[...]).astype(jnp.bfloat16)
        found = jnp.dot(table[...], slot[...], preferred_element_type=jnp.float32)
        for side in range(2):
            spectra[pl.ds(2 * pair + side, 2 * K, stride=WD), :] = found[:, side * CB : (side + 1) * CB]

    rows = 2 * KL * WD

    def add(f, power):
        part = spectra[pl.ds(pl.multiple_of(f * rows, rows), rows), :].reshape(2 * KL, WD, CB)
        return power + jnp.sum(part * part, axis=0)

    power = lax.fori_loop(0, NF, add, jnp.zeros((WD, CB), jnp.float32))
    gain = lax.rsqrt(power * (1.0 / (2 * K)) + 1e-6)[None]

    def whiten(f, carry):
        for out, which in ((near, half[0]), (other, 1 - half[0])):
            start = pl.multiple_of(f * rows + which * (rows // 2), rows // 2)
            part = spectra[pl.ds(start, rows // 2), :].reshape(KL, WD, CB)
            out[f] = (part * gain).astype(jnp.bfloat16).reshape(HB, 2, WD, CB)
        return carry

    lax.fori_loop(0, NF, whiten, 0)


def front(traces, kept_bins, window_starts, half):
    taper = 0.5 - 0.5 * jnp.cos(jnp.arange(L, dtype=jnp.float32) * (2.0 * math.pi / L))
    taper = jnp.broadcast_to(taper[:, None], (L, CB))
    bins = jnp.repeat(kept_bins, 2)[:, None]
    vmem = pl.BlockSpec(memory_space=pltpu.VMEM)
    smem = pl.BlockSpec(memory_space=pltpu.SMEM)
    piece = jax.ShapeDtypeStruct((NF, HB, 2, WD, CB), jnp.bfloat16)
    return pl.pallas_call(
        front_kernel,
        out_shape=(piece, piece),
        in_specs=[smem, smem, vmem, vmem, vmem],
        out_specs=(vmem, vmem),
        scratch_shapes=[
            pltpu.VMEM((SEG, CB), jnp.float32),
            pltpu.VMEM((2 * K, L), jnp.bfloat16),
            pltpu.VMEM((2, L, 2 * CB), jnp.bfloat16),
            pltpu.VMEM((2 * K * WD, CB), jnp.float32),
        ],
        compiler_params=pltpu.CompilerParams(vmem_limit_bytes=40 * MIB),
        name="white",
    )(window_starts, half, bins, taper, traces)


def left_side(ref):
    return jnp.concatenate([ref[:, 0, e].reshape(NF * WD, CB) for e in range(2)], axis=0)


def right_side(ref):
    real, imag = (ref[:, 0, e].reshape(NF * WD, CB) for e in range(2))
    return jnp.concatenate([jnp.concatenate([real, imag], axis=0), jnp.concatenate([-imag, real], axis=0)], axis=1)


def cross(left, right):
    found = lax.dot_general(left, right, (((0,), (0,)), ((), ())), preferred_element_type=jnp.float32)
    return (found * SCALE).astype(jnp.bfloat16)


def rounds_kernel(half, own, own_swapped, far, far_swapped, *rest):
    out = rest[-1]
    left = left_side(own)
    for r, ref in enumerate((own_swapped, far, far_swapped)):
        found = cross(left, right_side(ref))
        for e in range(2):
            out[r, e, 0] = found[:, e * CB : (e + 1) * CB]


def rounds(half, own, own_swapped, far, far_swapped, base=None):
    piece = pl.BlockSpec((NF, 1, 2, WD, CB), lambda k, half: (0, k, 0, 0, 0))
    given = [own, own_swapped, far, far_swapped]
    specs = [piece] * 4
    aliases = {}
    if base is not None:
        given.append(base)
        specs.append(pl.BlockSpec(memory_space=pl.ANY))
        aliases = {5: 0}
    return pl.pallas_call(
        rounds_kernel,
        out_shape=jax.ShapeDtypeStruct((4, 2, KL, CB, CB), jnp.bfloat16),
        grid_spec=pltpu.PrefetchScalarGridSpec(
            num_scalar_prefetch=1,
            grid=(HB,),
            in_specs=specs,
            out_specs=pl.BlockSpec((3, 2, 1, CB, CB), lambda k, half: (0, 0, half[0] * HB + k, 0, 0)),
        ),
        input_output_aliases=aliases,
        compiler_params=pltpu.CompilerParams(vmem_limit_bytes=40 * MIB),
        name="rounds",
    )(half, *given)


def between_kernel(far, side, to_far, to_side):
    for out, a, b in ((to_far, far, side), (to_side, side, far)):
        found = cross(left_side(a), right_side(b))
        for e in range(2):
            out[e, 0] = found[:, e * CB : (e + 1) * CB]


def between(far, side):
    piece = pl.BlockSpec((NF, 1, 2, WD, CB), lambda k: (0, k, 0, 0, 0))
    out = pl.BlockSpec((2, 1, CB, CB), lambda k: (0, k, 0, 0))
    shape = jax.ShapeDtypeStruct((2, HB, CB, CB), jnp.bfloat16)
    return pl.pallas_call(
        between_kernel,
        out_shape=(shape, shape),
        grid=(HB,),
        in_specs=[piece, piece],
        out_specs=(out, out),
        compiler_params=pltpu.CompilerParams(vmem_limit_bytes=40 * MIB),
        name="between",
    )(far, side)


def place_kernel(half, first, second, base, out, sems):
    copies = []
    for ref, which, n in ((first, half[0], 0), (second, 1 - half[0], 1)):
        copies.append(pltpu.make_async_copy(ref, out.at[3, :, pl.ds(which * HB, HB)], sems.at[n]))
    for copy in copies:
        copy.start()
    for copy in copies:
        copy.wait()


def place(half, first, second, base):
    anywhere = pl.BlockSpec(memory_space=pl.ANY)
    return pl.pallas_call(
        place_kernel,
        out_shape=jax.ShapeDtypeStruct(base.shape, base.dtype),
        in_specs=[pl.BlockSpec(memory_space=pltpu.SMEM), anywhere, anywhere, anywhere],
        out_specs=anywhere,
        scratch_shapes=[pltpu.SemaphoreType.DMA((2,))],
        input_output_aliases={3: 0},
        name="place",
    )(half, first, second, base)


def partner(block, mask):
    count = lax.axis_size("chan")
    return lax.ppermute(block, "chan", [(i, i ^ mask) for i in range(count)])


def turn(piece):
    return lax.all_to_all(piece, "freq", split_axis=0, concat_axis=0, tiled=True)


def together(*arrays):
    return lax.optimization_barrier(arrays)


def per_device(traces, kept_bins, window_starts):
    half = ((lax.axis_index("chan") >> 2) & 1).astype(jnp.int32).reshape(1)
    near, other = front(traces, kept_bins, window_starts, half)
    own_near = turn(near)
    far_near = partner(own_near, 2)
    other, _ = together(other, own_near)
    own_other = turn(other)
    side = partner(own_other, 6)
    far_other = partner(own_other, 2)
    far_near, side = together(far_near, side)
    to_far, to_side = between(far_near, side)
    first, second = partner(to_far, 2), partner(to_side, 6)
    base = rounds(half, own_near, partner(own_near, 1), far_near, partner(far_near, 1))
    base = rounds(1 - half, own_other, partner(own_other, 1), far_other, partner(far_other, 1), base)
    return place(half, first, second, base)


def solution(mesh):
    return jax.shard_map(
        per_device,
        mesh=mesh,
        in_specs=(P("freq", "chan"), P(), P("freq")),
        out_specs=P(None, None, "freq", "chan", None),
        check_vma=False,
    )
```

```python
import functools
import math

import jax
import jax.numpy as jnp
from jax import lax
from jax.experimental import pallas as pl
from jax.experimental.pallas import tpu as pltpu
from jax.sharding import PartitionSpec as P

L = 1024
K = 128
WD = 16
SEG = 8704
CB = 128
ROUNDS = 4
NF = 16
KL = K // NF
NX = 4
NZ = 4
HB = KL // 2
SCALE = 1.0 / math.sqrt(NF * WD)
MIB = 1 << 20

SIN_TERMS = [(-1) ** i * (2.0 * math.pi) ** (2 * i + 1) / math.factorial(2 * i + 1) for i in range(7)]


def cosine(phase):
    folded = jnp.minimum(phase, L - phase) - L // 4
    turn = folded.astype(jnp.float32) * (1.0 / L)
    square = turn * turn
    total = jnp.full(phase.shape, SIN_TERMS[-1], jnp.float32)
    for term in SIN_TERMS[-2::-1]:
        total = total * square + term
    return -(total * turn)


def front_kernel(position, starts_in, bins_in, traces, white, *refs):
    crossed, (starts, bins, held, wide, taper, table, tapered, spectra, ready, sems, out_sems) = refs[:NX], refs[NX:]
    copies = [
        pltpu.make_async_copy(bins_in, bins, sems.at[0]),
        pltpu.make_async_copy(starts_in, starts, sems.at[1]),
        pltpu.make_async_copy(traces, held, sems.at[2]),
    ]
    for copy in copies:
        copy.start()
    taper[...] = 0.5 - 0.5 * cosine(lax.broadcasted_iota(jnp.int32, (L, CB), 0))
    copies[0].wait()
    bin_rows = jnp.broadcast_to(bins[...].astype(jnp.float32), (K, K)).T.astype(jnp.int32)
    for block in range(L // K):
        sample = lax.broadcasted_iota(jnp.int32, (K, K), 1) + block * K
        for part in range(2):
            phase = (bin_rows * sample + part * (L // 4)) & (L - 1)
            table[part * K : (part + 1) * K, block * K : (block + 1) * K] = cosine(phase).astype(jnp.bfloat16)
    copies[1].wait()
    copies[2].wait()
    wide[...] = held[...].astype(jnp.float32)
    for pair in range(WD // 2):
        slot = tapered.at[pair % 2]
        for side in range(2):
            first = starts[2 * pair + side]
            mean = jnp.sum(wide[pl.ds(first, L), :], axis=0, keepdims=True) * (1.0 / L)
            slot[:, side * CB : (side + 1) * CB] = ((wide[pl.ds(first, L), :] - mean) * taper[...]).astype(jnp.bfloat16)
        found = jnp.dot(table[...], slot[...], preferred_element_type=jnp.float32)
        for side in range(2):
            for part in range(2):
                first_row = part * WD + 2 * pair + side
                spectra[pl.ds(first_row, K, stride=2 * WD), :] = found[part * K : (part + 1) * K, side * CB : (side + 1) * CB]

    rows = 2 * KL * WD

    def add(f, power):
        part = spectra[pl.ds(pl.multiple_of(f * rows, rows), rows), :].reshape(2 * KL, WD, CB)
        return power + jnp.sum(part * part, axis=0)

    power = lax.fori_loop(0, NF, add, jnp.zeros((WD, CB), jnp.float32))
    gain = lax.rsqrt(power * (1.0 / (2 * K)) + 1e-6)[None]

    def whiten(f, carry):
        for h in range(2):
            first = pl.multiple_of(f * rows + (position[0] ^ h) * (rows // 2), rows // 2)
            part = spectra[pl.ds(first, rows // 2), :].reshape(KL, WD, CB)
            ready[f, h * HB : (h + 1) * HB] = (part * gain).astype(jnp.bfloat16).reshape(HB, 2, WD, CB)
        for number in range(2):
            pltpu.make_async_copy(ready.at[f], white.at[number, f], out_sems.at[number]).start()
        return carry

    lax.fori_loop(0, NF, whiten, 0)
    for e, out in enumerate(crossed):
        for d in range(NZ):
            out[d] = ready[(d * NX + e) ^ position[1], HB:]
    for number in range(2):
        pltpu.make_async_copy(ready, white.at[number], out_sems.at[number]).wait()


def front(traces, kept_bins, window_starts, position):
    vmem = pl.BlockSpec(memory_space=pltpu.VMEM)
    smem = pl.BlockSpec(memory_space=pltpu.SMEM)
    hbm = pl.BlockSpec(memory_space=pltpu.HBM)
    given = [window_starts, kept_bins.reshape(1, K), traces]
    given = [pltpu.with_memory_space_constraint(array, pltpu.HBM) for array in given]
    return pl.pallas_call(
        front_kernel,
        out_shape=(pltpu.HBM((2, NF, KL, 2, WD, CB), jnp.bfloat16),)
        + (jax.ShapeDtypeStruct((NZ, HB, 2, WD, CB), jnp.bfloat16),) * NX,
        in_specs=[smem, hbm, hbm, hbm],
        out_specs=(hbm,) + (vmem,) * NX,
        scratch_shapes=[
            pltpu.SMEM((WD,), jnp.int32),
            pltpu.VMEM((1, K), jnp.int32),
            pltpu.VMEM((SEG, CB), jnp.bfloat16),
            pltpu.VMEM((SEG, CB), jnp.float32),
            pltpu.VMEM((L, CB), jnp.float32),
            pltpu.VMEM((2 * K, L), jnp.bfloat16),
            pltpu.VMEM((2, L, 2 * CB), jnp.bfloat16),
            pltpu.VMEM((2 * K * WD, CB), jnp.float32),
            pltpu.VMEM((NF, KL, 2, WD, CB), jnp.bfloat16),
            pltpu.SemaphoreType.DMA((3,)),
            pltpu.SemaphoreType.DMA((2,)),
        ],
        compiler_params=pltpu.CompilerParams(vmem_limit_bytes=40 * MIB),
        name="white",
    )(position, *given)


def left_side(refs):
    return jnp.concatenate([part_of(refs, 0), part_of(refs, 1)], axis=0)


def part_of(refs, e):
    parts = [ref[..., e, :, :].reshape(-1, CB) for ref in refs]
    return parts[0] if len(parts) == 1 else jnp.concatenate(parts, axis=0)


def right_side(refs):
    real, imag = part_of(refs, 0), part_of(refs, 1)
    return jnp.concatenate([jnp.concatenate([real, imag], axis=0), jnp.concatenate([-imag, real], axis=0)], axis=1)


def cross(left, right):
    found = lax.dot_general(left, right, (((0,), (0,)), ((), ())), preferred_element_type=jnp.float32)
    return (found * SCALE).astype(jnp.bfloat16)


def rounds_kernel(position, own, far, own_swapped, far_swapped, out):
    left = left_side([own])
    for r, ref in enumerate((own_swapped, far, far_swapped)):
        found = cross(left, right_side([ref]))
        for e in range(2):
            out[r, e, 0] = found[:, e * CB : (e + 1) * CB]


def rounds(position, both, both_swapped):
    own = pl.BlockSpec((1, NF, 1, 2, WD, CB), lambda k, position: (position[2], 0, k, 0, 0, 0))
    far = pl.BlockSpec((1, NF, 1, 2, WD, CB), lambda k, position: (1 - position[2], 0, k, 0, 0, 0))
    return pl.pallas_call(
        rounds_kernel,
        out_shape=jax.ShapeDtypeStruct((ROUNDS, 2, KL, CB, CB), jnp.bfloat16),
        grid_spec=pltpu.PrefetchScalarGridSpec(
            num_scalar_prefetch=1,
            grid=(KL,),
            in_specs=[own, far, own, far],
            out_specs=pl.BlockSpec((3, 2, 1, CB, CB), lambda k, position: (0, 0, k ^ (position[0] * HB), 0, 0)),
        ),
        compiler_params=pltpu.CompilerParams(vmem_limit_bytes=40 * MIB),
        name="rounds",
    )(position, both, both, both_swapped, both_swapped)


def between_kernel(position, *refs):
    far, side, (to_far, to_side) = refs[:NF], refs[NF : NF + NZ], refs[NF + NZ :]
    for out, a, b in ((to_far, far, side), (to_side, side, far)):
        found = cross(left_side(a), right_side(b))
        for e in range(2):
            out[e, 0] = found[:, e * CB : (e + 1) * CB]


def between(position, both, side):
    far = [
        pl.BlockSpec((1, 1, 1, 2, WD, CB), lambda k, position, g=g: (1 - position[2], g ^ position[1], k, 0, 0, 0))
        for g in range(NF)
    ]
    piece = pl.BlockSpec((NX, 1, 2, WD, CB), lambda k, position: (0, k, 0, 0, 0))
    out = pl.BlockSpec((2, 1, CB, CB), lambda k, position: (0, k, 0, 0))
    shape = jax.ShapeDtypeStruct((2, HB, CB, CB), jnp.bfloat16)
    return pl.pallas_call(
        between_kernel,
        out_shape=(shape, shape),
        grid_spec=pltpu.PrefetchScalarGridSpec(
            num_scalar_prefetch=1, grid=(HB,), in_specs=far + [piece] * NZ, out_specs=(out, out)
        ),
        compiler_params=pltpu.CompilerParams(vmem_limit_bytes=40 * MIB),
        name="between",
    )(position, *[both] * NF, *side)


def place_kernel(position, first, second, base, out):
    @pl.when(pl.program_id(0) == 0)
    def _():
        out[0] = first[...]

    @pl.when(pl.program_id(0) == 1)
    def _():
        out[0] = second[...]


def place(position, first, second, base):
    whole = pl.BlockSpec((2, HB, CB, CB), lambda step, half: (0, 0, 0, 0))
    return pl.pallas_call(
        place_kernel,
        out_shape=jax.ShapeDtypeStruct(base.shape, base.dtype),
        grid_spec=pltpu.PrefetchScalarGridSpec(
            num_scalar_prefetch=1,
            grid=(2,),
            in_specs=[whole, whole, pl.BlockSpec(memory_space=pl.ANY)],
            out_specs=pl.BlockSpec((1, 2, HB, CB, CB), lambda step, position: (3, 0, position[0] ^ step, 0, 0)),
        ),
        input_output_aliases={3: 0},
        compiler_params=pltpu.CompilerParams(vmem_limit_bytes=40 * MIB),
        name="place",
    )(position, first, second, base)


def partner(block, mask):
    count = lax.axis_size("chan")
    return lax.ppermute(block, "chan", [(i, i ^ mask) for i in range(count)])


def send(block, chan_mask, freq_mask):
    moves = []
    for c in range(lax.axis_size("chan")):
        for f in range(NF):
            moves.append((c * NF + f, (c ^ chan_mask) * NF + (f ^ freq_mask)))
    return lax.ppermute(block, ("chan", "freq"), moves)


def together(*arrays):
    return lax.optimization_barrier(arrays)


def pair_groups(mask):
    pairs = [(c, c ^ mask) for c in range(lax.axis_size("chan")) if c < c ^ mask]
    return [[c * NF + f for c in pair for f in range(NF)] for pair in pairs]


def per_device(traces, kept_bins, window_starts):
    chan, freq = lax.axis_index("chan"), lax.axis_index("freq")
    position = jnp.stack([(chan >> 2) & 1, freq, (chan >> 1) & 1]).astype(jnp.int32)
    white, *crossed = front(traces, kept_bins, window_starts, position)
    crossed = [crossed[0]] + [send(crossed[e], 0, e) for e in range(1, NX)]
    crossed = [jnp.stack([piece[d] for piece in crossed]) for d in range(NZ)]
    side = [send(crossed[d], 6, d * NX) for d in range(NZ)]
    both = lax.all_to_all(
        white.reshape((2 * NF,) + white.shape[2:]),
        ("chan", "freq"),
        split_axis=0,
        concat_axis=0,
        tiled=True,
        axis_index_groups=pair_groups(2),
    ).reshape(white.shape)
    both, *side = together(both, *side)
    to_far, to_side = between(position, both, side)
    first, second = partner(to_far, 2), partner(to_side, 6)
    base = rounds(position, both, partner(both, 1))
    return place(position, first, second, base)


def solution(mesh):
    return jax.shard_map(
        per_device,
        mesh=mesh,
        in_specs=(P("freq", "chan"), P(), P("freq")),
        out_specs=P(None, None, "freq", "chan", None),
        check_vma=False,
    )
```

```python
import functools
import math

import jax
import jax.numpy as jnp
from jax import lax
from jax.experimental import pallas as pl
from jax.experimental.pallas import tpu as pltpu
from jax.sharding import PartitionSpec as P

L = 1024
K = 128
WD = 16
SEG = 8704
CB = 128
ROUNDS = 4
NF = 16
KL = K // NF
NX = 4
NZ = 4
HB = KL // 2
SCALE = 1.0 / math.sqrt(NF * WD)
MIB = 1 << 20

SIN_TERMS = [(-1) ** i * (2.0 * math.pi) ** (2 * i + 1) / math.factorial(2 * i + 1) for i in range(7)]


def cosine(phase):
    folded = jnp.minimum(phase, L - phase) - L // 4
    turn = folded.astype(jnp.float32) * (1.0 / L)
    square = turn * turn
    total = jnp.full(phase.shape, SIN_TERMS[-1], jnp.float32)
    for term in SIN_TERMS[-2::-1]:
        total = total * square + term
    return -(total * turn)


def front_kernel(position, starts_in, bins_in, traces, white, *refs):
    crossed, (starts, bins, held, wide, taper, table, tapered, spectra, ready, sems, out_sems) = refs[:NX], refs[NX:]
    copies = [
        pltpu.make_async_copy(bins_in, bins, sems.at[0]),
        pltpu.make_async_copy(starts_in, starts, sems.at[1]),
        pltpu.make_async_copy(traces, held, sems.at[2]),
    ]
    for copy in copies:
        copy.start()
    taper[...] = 0.5 - 0.5 * cosine(lax.broadcasted_iota(jnp.int32, (L, CB), 0))
    copies[0].wait()
    bin_rows = jnp.broadcast_to(bins[...].astype(jnp.float32), (K, K)).T.astype(jnp.int32)
    for block in range(L // K):
        sample = lax.broadcasted_iota(jnp.int32, (K, K), 1) + block * K
        for part in range(2):
            phase = (bin_rows * sample + part * (L // 4)) & (L - 1)
            table[part * K : (part + 1) * K, block * K : (block + 1) * K] = cosine(phase).astype(jnp.bfloat16)
    copies[1].wait()
    copies[2].wait()
    wide[...] = held[...].astype(jnp.float32)
    for pair in range(WD // 2):
        slot = tapered.at[pair % 2]
        for side in range(2):
            first = starts[2 * pair + side]
            mean = jnp.sum(wide[pl.ds(first, L), :], axis=0, keepdims=True) * (1.0 / L)
            slot[:, side * CB : (side + 1) * CB] = ((wide[pl.ds(first, L), :] - mean) * taper[...]).astype(jnp.bfloat16)
        found = jnp.dot(table[...], slot[...], preferred_element_type=jnp.float32)
        for side in range(2):
            for part in range(2):
                first_row = part * WD + 2 * pair + side
                spectra[pl.ds(first_row, K, stride=2 * WD), :] = found[part * K : (part + 1) * K, side * CB : (side + 1) * CB]

    rows = 2 * KL * WD

    def add(f, power):
        part = spectra[pl.ds(pl.multiple_of(f * rows, rows), rows), :].reshape(2 * KL, WD, CB)
        return power + jnp.sum(part * part, axis=0)

    power = lax.fori_loop(0, NF, add, jnp.zeros((WD, CB), jnp.float32))
    gain = lax.rsqrt(power * (1.0 / (2 * K)) + 1e-6)[None]

    def whiten(f, carry):
        for h in range(2):
            first = pl.multiple_of(f * rows + (position[0] ^ h) * (rows // 2), rows // 2)
            part = spectra[pl.ds(first, rows // 2), :].reshape(KL, WD, CB)
            ready[f, h * HB : (h + 1) * HB] = (part * gain).astype(jnp.bfloat16).reshape(HB, 2, WD, CB)
        for number in range(2):
            pltpu.make_async_copy(ready.at[f], white.at[number, f], out_sems.at[number]).start()
        return carry

    lax.fori_loop(0, NF, whiten, 0)
    for e, out in enumerate(crossed):
        for d in range(NZ):
            out[d] = ready[(d * NX + e) ^ position[1], HB:]
    for number in range(2):
        pltpu.make_async_copy(ready, white.at[number], out_sems.at[number]).wait()


def front(traces, kept_bins, window_starts, position):
    vmem = pl.BlockSpec(memory_space=pltpu.VMEM)
    smem = pl.BlockSpec(memory_space=pltpu.SMEM)
    hbm = pl.BlockSpec(memory_space=pltpu.HBM)
    given = [window_starts, kept_bins.reshape(1, K), traces]
    given = [pltpu.with_memory_space_constraint(array, pltpu.HBM) for array in given]
    return pl.pallas_call(
        front_kernel,
        out_shape=(pltpu.HBM((2, NF, KL, 2, WD, CB), jnp.bfloat16),)
        + (jax.ShapeDtypeStruct((NZ, HB, 2, WD, CB), jnp.bfloat16),) * NX,
        in_specs=[smem, hbm, hbm, hbm],
        out_specs=(hbm,) + (vmem,) * NX,
        scratch_shapes=[
            pltpu.SMEM((WD,), jnp.int32),
            pltpu.VMEM((1, K), jnp.int32),
            pltpu.VMEM((SEG, CB), jnp.bfloat16),
            pltpu.VMEM((SEG, CB), jnp.float32),
            pltpu.VMEM((L, CB), jnp.float32),
            pltpu.VMEM((2 * K, L), jnp.bfloat16),
            pltpu.VMEM((2, L, 2 * CB), jnp.bfloat16),
            pltpu.VMEM((2 * K * WD, CB), jnp.float32),
            pltpu.VMEM((NF, KL, 2, WD, CB), jnp.bfloat16),
            pltpu.SemaphoreType.DMA((3,)),
            pltpu.SemaphoreType.DMA((2,)),
        ],
        compiler_params=pltpu.CompilerParams(vmem_limit_bytes=40 * MIB),
        name="white",
    )(position, *given)


def left_side(refs):
    return jnp.concatenate([part_of(refs, 0), part_of(refs, 1)], axis=0)


def part_of(refs, e):
    parts = [ref[..., e, :, :].reshape(-1, CB) for ref in refs]
    return parts[0] if len(parts) == 1 else jnp.concatenate(parts, axis=0)


def right_side(refs):
    real, imag = part_of(refs, 0), part_of(refs, 1)
    return jnp.concatenate([jnp.concatenate([real, imag], axis=0), jnp.concatenate([-imag, real], axis=0)], axis=1)


def cross(left, right):
    found = lax.dot_general(left, right, (((0,), (0,)), ((), ())), preferred_element_type=jnp.float32)
    return (found * SCALE).astype(jnp.bfloat16)


def rounds_kernel(position, own, far, own_swapped, far_swapped, out):
    left = left_side([own])
    for r, ref in enumerate((own_swapped, far, far_swapped)):
        found = cross(left, right_side([ref]))
        for e in range(2):
            out[r, e, 0] = found[:, e * CB : (e + 1) * CB]


def rounds(position, both, both_swapped):
    own = pl.BlockSpec((1, NF, 1, 2, WD, CB), lambda k, position: (position[2], 0, k, 0, 0, 0))
    far = pl.BlockSpec((1, NF, 1, 2, WD, CB), lambda k, position: (1 - position[2], 0, k, 0, 0, 0))
    return pl.pallas_call(
        rounds_kernel,
        out_shape=jax.ShapeDtypeStruct((ROUNDS, 2, KL, CB, CB), jnp.bfloat16),
        grid_spec=pltpu.PrefetchScalarGridSpec(
            num_scalar_prefetch=1,
            grid=(KL,),
            in_specs=[own, far, own, far],
            out_specs=pl.BlockSpec((3, 2, 1, CB, CB), lambda k, position: (0, 0, k ^ (position[0] * HB), 0, 0)),
        ),
        compiler_params=pltpu.CompilerParams(vmem_limit_bytes=40 * MIB),
        name="rounds",
    )(position, both, both, both_swapped, both_swapped)


def between_kernel(position, both, *refs):
    sides, (to_far, to_side) = refs[:NZ], refs[NZ:]
    for k in range(HB):
        far = [both.at[1 - position[2], g ^ position[1], k] for g in range(NF)]
        side = [ref.at[:, k] for ref in sides]
        for out, a, b in ((to_far, far, side), (to_side, side, far)):
            found = cross(left_side(a), right_side(b))
            for e in range(2):
                out[e, k] = found[:, e * CB : (e + 1) * CB]


def between(position, both, side):
    vmem = pl.BlockSpec(memory_space=pltpu.VMEM)
    shape = jax.ShapeDtypeStruct((2, HB, CB, CB), jnp.bfloat16)
    return pl.pallas_call(
        between_kernel,
        out_shape=(shape, shape),
        in_specs=[pl.BlockSpec(memory_space=pltpu.SMEM)] + [vmem] * (1 + NZ),
        out_specs=(vmem, vmem),
        compiler_params=pltpu.CompilerParams(vmem_limit_bytes=40 * MIB),
        name="between",
    )(position, both, *side)


def place_kernel(position, first, second, base, out):
    @pl.when(pl.program_id(0) == 0)
    def _():
        out[0] = first[...]

    @pl.when(pl.program_id(0) == 1)
    def _():
        out[0] = second[...]


def place(position, first, second, base):
    whole = pl.BlockSpec((2, HB, CB, CB), lambda step, half: (0, 0, 0, 0))
    return pl.pallas_call(
        place_kernel,
        out_shape=jax.ShapeDtypeStruct(base.shape, base.dtype),
        grid_spec=pltpu.PrefetchScalarGridSpec(
            num_scalar_prefetch=1,
            grid=(2,),
            in_specs=[whole, whole, pl.BlockSpec(memory_space=pl.ANY)],
            out_specs=pl.BlockSpec((1, 2, HB, CB, CB), lambda step, position: (3, 0, position[0] ^ step, 0, 0)),
        ),
        input_output_aliases={3: 0},
        compiler_params=pltpu.CompilerParams(vmem_limit_bytes=40 * MIB),
        name="place",
    )(position, first, second, base)


def partner(block, mask):
    count = lax.axis_size("chan")
    return lax.ppermute(block, "chan", [(i, i ^ mask) for i in range(count)])


def send(block, chan_mask, freq_mask):
    moves = []
    for c in range(lax.axis_size("chan")):
        for f in range(NF):
            moves.append((c * NF + f, (c ^ chan_mask) * NF + (f ^ freq_mask)))
    return lax.ppermute(block, ("chan", "freq"), moves)


def together(*arrays):
    return lax.optimization_barrier(arrays)


def pair_groups(mask):
    pairs = [(c, c ^ mask) for c in range(lax.axis_size("chan")) if c < c ^ mask]
    return [[c * NF + f for c in pair for f in range(NF)] for pair in pairs]


def per_device(traces, kept_bins, window_starts):
    chan, freq = lax.axis_index("chan"), lax.axis_index("freq")
    position = jnp.stack([(chan >> 2) & 1, freq, (chan >> 1) & 1]).astype(jnp.int32)
    white, *crossed = front(traces, kept_bins, window_starts, position)
    crossed = [crossed[0]] + [send(crossed[e], 0, e) for e in range(1, NX)]
    crossed = [jnp.stack([piece[d] for piece in crossed]) for d in range(NZ)]
    side = [send(crossed[d], 6, d * NX) for d in range(NZ)]
    both = lax.all_to_all(
        white.reshape((2 * NF,) + white.shape[2:]),
        ("chan", "freq"),
        split_axis=0,
        concat_axis=0,
        tiled=True,
        axis_index_groups=pair_groups(2),
    ).reshape(white.shape)
    both, *side = together(both, *side)
    to_far, to_side = between(position, both, side)
    first, second = partner(to_far, 2), partner(to_side, 6)
    base = rounds(position, both, partner(both, 1))
    return place(position, first, second, base)


def solution(mesh):
    return jax.shard_map(
        per_device,
        mesh=mesh,
        in_specs=(P("freq", "chan"), P(), P("freq")),
        out_specs=P(None, None, "freq", "chan", None),
        check_vma=False,
    )
```

```python
import functools
import math

import jax
import jax.numpy as jnp
from jax import lax
from jax.experimental import pallas as pl
from jax.experimental.pallas import tpu as pltpu
from jax.sharding import PartitionSpec as P

L = 1024
K = 128
WD = 16
SEG = 8704
CB = 128
ROUNDS = 4
NF = 16
KL = K // NF
NX = 4
NZ = 4
HB = KL // 2
SCALE = 1.0 / math.sqrt(NF * WD)
MIB = 1 << 20

SIN_TERMS = [(-1) ** i * (2.0 * math.pi) ** (2 * i + 1) / math.factorial(2 * i + 1) for i in range(7)]


def cosine(phase):
    folded = jnp.minimum(phase, L - phase) - L // 4
    turn = folded.astype(jnp.float32) * (1.0 / L)
    square = turn * turn
    total = jnp.full(phase.shape, SIN_TERMS[-1], jnp.float32)
    for term in SIN_TERMS[-2::-1]:
        total = total * square + term
    return -(total * turn)


def front_kernel(position, starts_in, bins_in, traces, white, *refs):
    crossed, (starts, bins, held, wide, taper, table, tapered, spectra, ready, sems, out_sems) = refs[:NX], refs[NX:]
    copies = [
        pltpu.make_async_copy(bins_in, bins, sems.at[0]),
        pltpu.make_async_copy(starts_in, starts, sems.at[1]),
        pltpu.make_async_copy(traces, held, sems.at[2]),
    ]
    for copy in copies:
        copy.start()
    taper[...] = 0.5 - 0.5 * cosine(lax.broadcasted_iota(jnp.int32, (L, CB), 0))
    copies[0].wait()
    bin_rows = jnp.broadcast_to(bins[...].astype(jnp.float32), (K, K)).T.astype(jnp.int32)
    for block in range(L // K):
        sample = lax.broadcasted_iota(jnp.int32, (K, K), 1) + block * K
        for part in range(2):
            phase = (bin_rows * sample + part * (L // 4)) & (L - 1)
            table[part * K : (part + 1) * K, block * K : (block + 1) * K] = cosine(phase).astype(jnp.bfloat16)
    copies[1].wait()
    copies[2].wait()
    wide[:SEG, :] = held[...].astype(jnp.float32)
    wide[SEG:, :] = jnp.zeros((2 * WD, CB), jnp.float32)
    for pair in range(WD // 2):
        slot = tapered.at[pair % 2]
        for side in range(2):
            first = starts[2 * pair + side]
            mean = jnp.sum(wide[pl.ds(first, L), :], axis=0, keepdims=True) * (1.0 / L)
            slot[:, side * CB : (side + 1) * CB] = ((wide[pl.ds(first, L), :] - mean) * taper[...]).astype(jnp.bfloat16)
        found = jnp.dot(table[...], slot[...], preferred_element_type=jnp.float32)
        for side in range(2):
            for part in range(2):
                first_row = part * WD + 2 * pair + side
                spectra[pl.ds(first_row, K, stride=2 * WD), :] = found[part * K : (part + 1) * K, side * CB : (side + 1) * CB]

    rows = 2 * KL * WD

    def add(f, power):
        part = spectra[pl.ds(pl.multiple_of(f * rows, rows), rows), :].reshape(2 * KL, WD, CB)
        return power + jnp.sum(part * part, axis=0)

    power = lax.fori_loop(0, NF, add, jnp.zeros((WD, CB), jnp.float32), unroll=4)
    gain = lax.rsqrt(power * (1.0 / (2 * K)) + 1e-6)[None]

    def whiten(f, carry):
        for h in range(2):
            first = pl.multiple_of(f * rows + (position[0] ^ h) * (rows // 2), rows // 2)
            part = spectra[pl.ds(first, rows // 2), :].reshape(KL, WD, CB)
            ready[f, h * HB : (h + 1) * HB] = (part * gain).astype(jnp.bfloat16).reshape(HB, 2, WD, CB)
        for number in range(2):
            pltpu.make_async_copy(ready.at[f], white.at[number, f], out_sems.at[number]).start()
        return carry

    lax.fori_loop(0, NF, whiten, 0, unroll=4)
    for e, out in enumerate(crossed):
        for d in range(NZ):
            out[d] = ready[(d * NX + e) ^ position[1], HB:]
    for number in range(2):
        pltpu.make_async_copy(ready, white.at[number], out_sems.at[number]).wait()


def front(traces, kept_bins, window_starts, position):
    vmem = pl.BlockSpec(memory_space=pltpu.VMEM)
    smem = pl.BlockSpec(memory_space=pltpu.SMEM)
    hbm = pl.BlockSpec(memory_space=pltpu.HBM)
    given = [window_starts, kept_bins.reshape(1, K), traces]
    given = [pltpu.with_memory_space_constraint(array, pltpu.HBM) for array in given]
    return pl.pallas_call(
        front_kernel,
        out_shape=(pltpu.HBM((2, NF, KL, 2, WD, CB), jnp.bfloat16),)
        + (jax.ShapeDtypeStruct((NZ, HB, 2, WD, CB), jnp.bfloat16),) * NX,
        in_specs=[smem, hbm, hbm, hbm],
        out_specs=(hbm,) + (vmem,) * NX,
        scratch_shapes=[
            pltpu.SMEM((WD,), jnp.int32),
            pltpu.VMEM((1, K), jnp.int32),
            pltpu.VMEM((SEG, CB), jnp.bfloat16),
            pltpu.VMEM((SEG + 2 * WD, CB), jnp.float32),
            pltpu.VMEM((L, CB), jnp.float32),
            pltpu.VMEM((2 * K, L), jnp.bfloat16),
            pltpu.VMEM((2, L, 2 * CB), jnp.bfloat16),
            pltpu.VMEM((2 * K * WD + 2 * WD, CB), jnp.float32),
            pltpu.VMEM((NF, KL, 2, WD, CB), jnp.bfloat16),
            pltpu.SemaphoreType.DMA((3,)),
            pltpu.SemaphoreType.DMA((2,)),
        ],
        compiler_params=pltpu.CompilerParams(vmem_limit_bytes=40 * MIB),
        name="white",
    )(position, *given)


def left_side(refs):
    return jnp.concatenate([part_of(refs, 0), part_of(refs, 1)], axis=0)


def part_of(refs, e):
    parts = [ref[..., e, :, :].reshape(-1, CB) for ref in refs]
    return parts[0] if len(parts) == 1 else jnp.concatenate(parts, axis=0)


def right_side(refs):
    real, imag = part_of(refs, 0), part_of(refs, 1)
    return jnp.concatenate([jnp.concatenate([real, imag], axis=0), jnp.concatenate([-imag, real], axis=0)], axis=1)


def cross(left, right):
    found = lax.dot_general(left, right, (((0,), (0,)), ((), ())), preferred_element_type=jnp.float32)
    return (found * SCALE).astype(jnp.bfloat16)


def rounds_kernel(position, own, far, own_swapped, far_swapped, out):
    left = left_side([own])
    for r, ref in enumerate((own_swapped, far, far_swapped)):
        found = cross(left, right_side([ref]))
        for e in range(2):
            out[r, e, 0] = found[:, e * CB : (e + 1) * CB]


def rounds(position, both, both_swapped):
    own = pl.BlockSpec((1, NF, 1, 2, WD, CB), lambda k, position: (position[2], 0, k, 0, 0, 0))
    far = pl.BlockSpec((1, NF, 1, 2, WD, CB), lambda k, position: (1 - position[2], 0, k, 0, 0, 0))
    return pl.pallas_call(
        rounds_kernel,
        out_shape=jax.ShapeDtypeStruct((ROUNDS, 2, KL, CB, CB), jnp.bfloat16),
        grid_spec=pltpu.PrefetchScalarGridSpec(
            num_scalar_prefetch=1,
            grid=(KL,),
            in_specs=[own, far, own, far],
            out_specs=pl.BlockSpec((3, 2, 1, CB, CB), lambda k, position: (0, 0, k ^ (position[0] * HB), 0, 0)),
        ),
        compiler_params=pltpu.CompilerParams(vmem_limit_bytes=40 * MIB),
        name="rounds",
    )(position, both, both, both_swapped, both_swapped)


def between_kernel(position, both, *refs):
    sides, (to_far, to_side) = refs[:NZ], refs[NZ:]
    for k in range(HB):
        far = [both.at[1 - position[2], g ^ position[1], k] for g in range(NF)]
        side = [ref.at[:, k] for ref in sides]
        left, right = (jnp.concatenate([part_of(refs, 0), part_of(refs, 1)], axis=1) for refs in (far, side))
        found = lax.dot_general(left, right, (((0,), (0,)), ((), ())), preferred_element_type=jnp.float32)
        real = (found[:CB, :CB] + found[CB:, CB:]) * SCALE
        imag = (found[CB:, :CB] - found[:CB, CB:]) * SCALE
        to_far[0, k], to_far[1, k] = real.astype(jnp.bfloat16), imag.astype(jnp.bfloat16)
        to_side[0, k], to_side[1, k] = real.T.astype(jnp.bfloat16), (-imag).T.astype(jnp.bfloat16)


def between(position, both, side):
    vmem = pl.BlockSpec(memory_space=pltpu.VMEM)
    shape = jax.ShapeDtypeStruct((2, HB, CB, CB), jnp.bfloat16)
    return pl.pallas_call(
        between_kernel,
        out_shape=(shape, shape),
        in_specs=[pl.BlockSpec(memory_space=pltpu.SMEM)] + [vmem] * (1 + NZ),
        out_specs=(vmem, vmem),
        compiler_params=pltpu.CompilerParams(vmem_limit_bytes=40 * MIB),
        name="between",
    )(position, both, *side)


def place_kernel(position, first, second, base, out):
    @pl.when(pl.program_id(0) == 0)
    def _():
        out[0] = first[...]

    @pl.when(pl.program_id(0) == 1)
    def _():
        out[0] = second[...]


def place(position, first, second, base):
    whole = pl.BlockSpec((2, HB, CB, CB), lambda step, half: (0, 0, 0, 0))
    return pl.pallas_call(
        place_kernel,
        out_shape=jax.ShapeDtypeStruct(base.shape, base.dtype),
        grid_spec=pltpu.PrefetchScalarGridSpec(
            num_scalar_prefetch=1,
            grid=(2,),
            in_specs=[whole, whole, pl.BlockSpec(memory_space=pl.ANY)],
            out_specs=pl.BlockSpec((1, 2, HB, CB, CB), lambda step, position: (3, 0, position[0] ^ step, 0, 0)),
        ),
        input_output_aliases={3: 0},
        compiler_params=pltpu.CompilerParams(vmem_limit_bytes=40 * MIB),
        name="place",
    )(position, first, second, base)


def partner(block, mask):
    count = lax.axis_size("chan")
    return lax.ppermute(block, "chan", [(i, i ^ mask) for i in range(count)])


def send(block, chan_mask, freq_mask):
    moves = []
    for c in range(lax.axis_size("chan")):
        for f in range(NF):
            moves.append((c * NF + f, (c ^ chan_mask) * NF + (f ^ freq_mask)))
    return lax.ppermute(block, ("chan", "freq"), moves)


def together(*arrays):
    return lax.optimization_barrier(arrays)


def pair_groups(mask):
    pairs = [(c, c ^ mask) for c in range(lax.axis_size("chan")) if c < c ^ mask]
    return [[c * NF + f for c in pair for f in range(NF)] for pair in pairs]


def per_device(traces, kept_bins, window_starts):
    chan, freq = lax.axis_index("chan"), lax.axis_index("freq")
    position = jnp.stack([(chan >> 2) & 1, freq, (chan >> 1) & 1]).astype(jnp.int32)
    white, *crossed = front(traces, kept_bins, window_starts, position)
    crossed = [crossed[0]] + [send(crossed[e], 0, e) for e in range(1, NX)]
    crossed = [jnp.stack([piece[d] for piece in crossed]) for d in range(NZ)]
    side = [send(crossed[d], 6, d * NX) for d in range(NZ)]
    both = lax.all_to_all(
        white.reshape((2 * NF,) + white.shape[2:]),
        ("chan", "freq"),
        split_axis=0,
        concat_axis=0,
        tiled=True,
        axis_index_groups=pair_groups(2),
    ).reshape(white.shape)
    both, *side = together(both, *side)
    to_far, to_side = between(position, both, side)
    first, second = partner(to_far, 2), partner(to_side, 6)
    base = rounds(position, both, partner(both, 1))
    return place(position, first, second, base)


def solution(mesh):
    return jax.shard_map(
        per_device,
        mesh=mesh,
        in_specs=(P("freq", "chan"), P(), P("freq")),
        out_specs=P(None, None, "freq", "chan", None),
        check_vma=False,
    )
```

```python
import functools
import math

import jax
import jax.numpy as jnp
from jax import lax
from jax.experimental import pallas as pl
from jax.experimental.pallas import tpu as pltpu
from jax.sharding import PartitionSpec as P

L = 1024
K = 128
WD = 16
SEG = 8704
CB = 128
ROUNDS = 4
NF = 16
KL = K // NF
NX = 4
NZ = 4
HB = KL // 2
SCALE = 1.0 / math.sqrt(NF * WD)
MIB = 1 << 20

SIN_TERMS = [(-1) ** i * (2.0 * math.pi) ** (2 * i + 1) / math.factorial(2 * i + 1) for i in range(7)]


def cosine(phase):
    folded = jnp.minimum(phase, L - phase) - L // 4
    turn = folded.astype(jnp.float32) * (1.0 / L)
    square = turn * turn
    total = jnp.full(phase.shape, SIN_TERMS[-1], jnp.float32)
    for term in SIN_TERMS[-2::-1]:
        total = total * square + term
    return -(total * turn)


def front_kernel(position, starts_in, bins_in, traces, white, *refs):
    crossed, (starts, bins, held, wide, taper, table, tapered, spectra, ready, sems, out_sems) = refs[:NX], refs[NX:]
    copies = [
        pltpu.make_async_copy(bins_in, bins, sems.at[0]),
        pltpu.make_async_copy(starts_in, starts, sems.at[1]),
        pltpu.make_async_copy(traces, held, sems.at[2]),
    ]
    for copy in copies:
        copy.start()
    taper[...] = 0.5 - 0.5 * cosine(lax.broadcasted_iota(jnp.int32, (L, CB), 0))
    copies[0].wait()
    bin_rows = jnp.broadcast_to(bins[...].astype(jnp.float32), (K, K)).T.astype(jnp.int32)
    for block in range(L // K):
        sample = lax.broadcasted_iota(jnp.int32, (K, K), 1) + block * K
        for part in range(2):
            phase = (bin_rows * sample + part * (L // 4)) & (L - 1)
            table[part * K : (part + 1) * K, block * K : (block + 1) * K] = cosine(phase).astype(jnp.bfloat16)
    copies[1].wait()
    copies[2].wait()
    wide[:SEG, :] = held[...].astype(jnp.float32)
    wide[SEG:, :] = jnp.zeros((2 * WD, CB), jnp.float32)
    for pair in range(WD // 2):
        slot = tapered.at[pair % 2]
        for side in range(2):
            first = starts[2 * pair + side]
            mean = jnp.sum(wide[pl.ds(first, L), :], axis=0, keepdims=True) * (1.0 / L)
            slot[:, side * CB : (side + 1) * CB] = ((wide[pl.ds(first, L), :] - mean) * taper[...]).astype(jnp.bfloat16)
        found = jnp.dot(table[...], slot[...], preferred_element_type=jnp.float32)
        for side in range(2):
            spectra[2 * pair + side] = found[:, side * CB : (side + 1) * CB]

    power = jnp.concatenate([jnp.sum(spectra[w] * spectra[w], axis=0, keepdims=True) for w in range(WD)], axis=0)
    gain = lax.rsqrt(power * (1.0 / (2 * K)) + 1e-6)[None]

    def whiten(f, carry):
        for e in range(2):
            part = spectra[:, pl.ds(pl.multiple_of(e * K + f * KL, KL), KL), :]
            part = (jnp.swapaxes(part, 0, 1) * gain).astype(jnp.bfloat16)
            for h in range(2):
                ready[f, pl.ds((position[0] ^ h) * HB, HB), e] = part[h * HB : (h + 1) * HB]
        for number in range(2):
            pltpu.make_async_copy(ready.at[f], white.at[number, f], out_sems.at[number]).start()
        return carry

    lax.fori_loop(0, NF, whiten, 0, unroll=4)
    for e, out in enumerate(crossed):
        for d in range(NZ):
            out[d] = ready[(d * NX + e) ^ position[1], HB:]
    for number in range(2):
        pltpu.make_async_copy(ready, white.at[number], out_sems.at[number]).wait()


def front(traces, kept_bins, window_starts, position):
    vmem = pl.BlockSpec(memory_space=pltpu.VMEM)
    smem = pl.BlockSpec(memory_space=pltpu.SMEM)
    hbm = pl.BlockSpec(memory_space=pltpu.HBM)
    given = [window_starts, kept_bins.reshape(1, K), traces]
    given = [pltpu.with_memory_space_constraint(array, pltpu.HBM) for array in given]
    return pl.pallas_call(
        front_kernel,
        out_shape=(pltpu.HBM((2, NF, KL, 2, WD, CB), jnp.bfloat16),)
        + (jax.ShapeDtypeStruct((NZ, HB, 2, WD, CB), jnp.bfloat16),) * NX,
        in_specs=[smem, hbm, hbm, hbm],
        out_specs=(hbm,) + (vmem,) * NX,
        scratch_shapes=[
            pltpu.SMEM((WD,), jnp.int32),
            pltpu.VMEM((1, K), jnp.int32),
            pltpu.VMEM((SEG, CB), jnp.bfloat16),
            pltpu.VMEM((SEG + 2 * WD, CB), jnp.float32),
            pltpu.VMEM((L, CB), jnp.float32),
            pltpu.VMEM((2 * K, L), jnp.bfloat16),
            pltpu.VMEM((2, L, 2 * CB), jnp.bfloat16),
            pltpu.VMEM((WD, 2 * K, CB), jnp.float32),
            pltpu.VMEM((NF, KL, 2, WD, CB), jnp.bfloat16),
            pltpu.SemaphoreType.DMA((3,)),
            pltpu.SemaphoreType.DMA((2,)),
        ],
        compiler_params=pltpu.CompilerParams(vmem_limit_bytes=40 * MIB),
        name="white",
    )(position, *given)


def left_side(refs):
    return jnp.concatenate([part_of(refs, 0), part_of(refs, 1)], axis=0)


def part_of(refs, e):
    parts = [ref[..., e, :, :].reshape(-1, CB) for ref in refs]
    return parts[0] if len(parts) == 1 else jnp.concatenate(parts, axis=0)


def right_side(refs):
    real, imag = part_of(refs, 0), part_of(refs, 1)
    return jnp.concatenate([jnp.concatenate([real, imag], axis=0), jnp.concatenate([-imag, real], axis=0)], axis=1)


def cross(left, right):
    found = lax.dot_general(left, right, (((0,), (0,)), ((), ())), preferred_element_type=jnp.float32)
    return (found * SCALE).astype(jnp.bfloat16)


def rounds_kernel(position, own, far, own_swapped, far_swapped, out):
    left = left_side([own])
    for r, ref in enumerate((own_swapped, far, far_swapped)):
        found = cross(left, right_side([ref]))
        for e in range(2):
            out[r, e, 0] = found[:, e * CB : (e + 1) * CB]


def rounds(position, both, both_swapped):
    own = pl.BlockSpec((1, NF, 1, 2, WD, CB), lambda k, position: (position[2], 0, k, 0, 0, 0))
    far = pl.BlockSpec((1, NF, 1, 2, WD, CB), lambda k, position: (1 - position[2], 0, k, 0, 0, 0))
    return pl.pallas_call(
        rounds_kernel,
        out_shape=jax.ShapeDtypeStruct((ROUNDS, 2, KL, CB, CB), jnp.bfloat16),
        grid_spec=pltpu.PrefetchScalarGridSpec(
            num_scalar_prefetch=1,
            grid=(KL,),
            in_specs=[own, far, own, far],
            out_specs=pl.BlockSpec((3, 2, 1, CB, CB), lambda k, position: (0, 0, k ^ (position[0] * HB), 0, 0)),
        ),
        compiler_params=pltpu.CompilerParams(vmem_limit_bytes=40 * MIB),
        name="rounds",
    )(position, both, both, both_swapped, both_swapped)


def between_kernel(position, both, *refs):
    sides, (to_far, to_side) = refs[:NZ], refs[NZ:]
    for k in range(HB):
        far = [both.at[1 - position[2], g ^ position[1], k] for g in range(NF)]
        side = [ref.at[:, k] for ref in sides]
        left, right = (jnp.concatenate([part_of(refs, 0), part_of(refs, 1)], axis=1) for refs in (far, side))
        found = lax.dot_general(left, right, (((0,), (0,)), ((), ())), preferred_element_type=jnp.float32)
        real = (found[:CB, :CB] + found[CB:, CB:]) * SCALE
        imag = (found[CB:, :CB] - found[:CB, CB:]) * SCALE
        to_far[0, k], to_far[1, k] = real.astype(jnp.bfloat16), imag.astype(jnp.bfloat16)
        to_side[0, k], to_side[1, k] = real.T.astype(jnp.bfloat16), (-imag).T.astype(jnp.bfloat16)


def between(position, both, side):
    vmem = pl.BlockSpec(memory_space=pltpu.VMEM)
    shape = jax.ShapeDtypeStruct((2, HB, CB, CB), jnp.bfloat16)
    return pl.pallas_call(
        between_kernel,
        out_shape=(shape, shape),
        in_specs=[pl.BlockSpec(memory_space=pltpu.SMEM)] + [vmem] * (1 + NZ),
        out_specs=(vmem, vmem),
        compiler_params=pltpu.CompilerParams(vmem_limit_bytes=40 * MIB),
        name="between",
    )(position, both, *side)


def place_kernel(position, first, second, base, out):
    @pl.when(pl.program_id(0) == 0)
    def _():
        out[0] = first[...]

    @pl.when(pl.program_id(0) == 1)
    def _():
        out[0] = second[...]


def place(position, first, second, base):
    whole = pl.BlockSpec((2, HB, CB, CB), lambda step, half: (0, 0, 0, 0))
    return pl.pallas_call(
        place_kernel,
        out_shape=jax.ShapeDtypeStruct(base.shape, base.dtype),
        grid_spec=pltpu.PrefetchScalarGridSpec(
            num_scalar_prefetch=1,
            grid=(2,),
            in_specs=[whole, whole, pl.BlockSpec(memory_space=pl.ANY)],
            out_specs=pl.BlockSpec((1, 2, HB, CB, CB), lambda step, position: (3, 0, position[0] ^ step, 0, 0)),
        ),
        input_output_aliases={3: 0},
        compiler_params=pltpu.CompilerParams(vmem_limit_bytes=40 * MIB),
        name="place",
    )(position, first, second, base)


def partner(block, mask):
    count = lax.axis_size("chan")
    return lax.ppermute(block, "chan", [(i, i ^ mask) for i in range(count)])


def send(block, chan_mask, freq_mask):
    moves = []
    for c in range(lax.axis_size("chan")):
        for f in range(NF):
            moves.append((c * NF + f, (c ^ chan_mask) * NF + (f ^ freq_mask)))
    return lax.ppermute(block, ("chan", "freq"), moves)


def together(*arrays):
    return lax.optimization_barrier(arrays)


def pair_groups(mask):
    pairs = [(c, c ^ mask) for c in range(lax.axis_size("chan")) if c < c ^ mask]
    return [[c * NF + f for c in pair for f in range(NF)] for pair in pairs]


def per_device(traces, kept_bins, window_starts):
    chan, freq = lax.axis_index("chan"), lax.axis_index("freq")
    position = jnp.stack([(chan >> 2) & 1, freq, (chan >> 1) & 1]).astype(jnp.int32)
    white, *crossed = front(traces, kept_bins, window_starts, position)
    crossed = [crossed[0]] + [send(crossed[e], 0, e) for e in range(1, NX)]
    crossed = [jnp.stack([piece[d] for piece in crossed]) for d in range(NZ)]
    side = [send(crossed[d], 6, d * NX) for d in range(NZ)]
    both = lax.all_to_all(
        white.reshape((2 * NF,) + white.shape[2:]),
        ("chan", "freq"),
        split_axis=0,
        concat_axis=0,
        tiled=True,
        axis_index_groups=pair_groups(2),
    ).reshape(white.shape)
    both, *side = together(both, *side)
    to_far, to_side = between(position, both, side)
    first, second = partner(to_far, 2), partner(to_side, 6)
    base = rounds(position, both, partner(both, 1))
    return place(position, first, second, base)


def solution(mesh):
    return jax.shard_map(
        per_device,
        mesh=mesh,
        in_specs=(P("freq", "chan"), P(), P("freq")),
        out_specs=P(None, None, "freq", "chan", None),
        check_vma=False,
    )
```

```python
import functools
import math

import jax
import jax.numpy as jnp
from jax import lax
from jax.experimental import pallas as pl
from jax.experimental.pallas import tpu as pltpu
from jax.sharding import PartitionSpec as P

L = 1024
K = 128
WD = 16
SEG = 8704
CB = 128
ROUNDS = 4
NF = 16
KL = K // NF
NX = 4
NZ = 4
HB = KL // 2
SCALE = 1.0 / math.sqrt(NF * WD)
MIB = 1 << 20

SIN_TERMS = [(-1) ** i * (2.0 * math.pi) ** (2 * i + 1) / math.factorial(2 * i + 1) for i in range(7)]


def cosine(phase):
    folded = jnp.minimum(phase, L - phase) - L // 4
    turn = folded.astype(jnp.float32) * (1.0 / L)
    square = turn * turn
    total = jnp.full(phase.shape, SIN_TERMS[-1], jnp.float32)
    for term in SIN_TERMS[-2::-1]:
        total = total * square + term
    return -(total * turn)


def front_kernel(position, starts_in, bins_in, traces, white, *refs):
    crossed, (starts, bins, held, wide, taper, table, tapered, spectra, ready, sems, out_sems) = refs[:NX], refs[NX:]
    copies = [
        pltpu.make_async_copy(bins_in, bins, sems.at[0]),
        pltpu.make_async_copy(starts_in, starts, sems.at[1]),
        pltpu.make_async_copy(traces, held, sems.at[2]),
    ]
    for copy in copies:
        copy.start()
    taper[...] = 0.5 - 0.5 * cosine(lax.broadcasted_iota(jnp.int32, (L, CB), 0))
    copies[0].wait()
    bin_rows = jnp.broadcast_to(bins[...].astype(jnp.float32), (K, K)).T.astype(jnp.int32)
    for block in range(L // K):
        sample = lax.broadcasted_iota(jnp.int32, (K, K), 1) + block * K
        for part in range(2):
            phase = (bin_rows * sample + part * (L // 4)) & (L - 1)
            table[part * K : (part + 1) * K, block * K : (block + 1) * K] = cosine(phase).astype(jnp.bfloat16)
    copies[1].wait()
    copies[2].wait()
    wide[:SEG, :] = held[...].astype(jnp.float32)
    wide[SEG:, :] = jnp.zeros((2 * WD, CB), jnp.float32)
    power = []
    for pair in range(WD // 2):
        slot = tapered.at[pair % 2]
        for side in range(2):
            first = starts[2 * pair + side]
            mean = jnp.sum(wide[pl.ds(first, L), :], axis=0, keepdims=True) * (1.0 / L)
            slot[:, side * CB : (side + 1) * CB] = ((wide[pl.ds(first, L), :] - mean) * taper[...]).astype(jnp.bfloat16)
        found = jnp.dot(table[...], slot[...], preferred_element_type=jnp.float32)
        for side in range(2):
            spectra[2 * pair + side] = found[:, side * CB : (side + 1) * CB]
        squares = jnp.sum(found * found, axis=0, keepdims=True)
        power += [squares[:, :CB], squares[:, CB:]]

    gain = lax.rsqrt(jnp.concatenate(power, axis=0) * (1.0 / (2 * K)) + 1e-6)[None]

    def whiten(f, carry):
        for e in range(2):
            part = spectra[:, pl.ds(pl.multiple_of(e * K + f * KL, KL), KL), :]
            part = (jnp.swapaxes(part, 0, 1) * gain).astype(jnp.bfloat16)
            for h in range(2):
                ready[f, pl.ds((position[0] ^ h) * HB, HB), e] = part[h * HB : (h + 1) * HB]
        for number in range(2):
            pltpu.make_async_copy(ready.at[f], white.at[number, f], out_sems.at[number]).start()
        return carry

    lax.fori_loop(0, NF, whiten, 0)
    for e, out in enumerate(crossed):
        for d in range(NZ):
            out[d] = ready[(d * NX + e) ^ position[1], HB:]
    for number in range(2):
        pltpu.make_async_copy(ready, white.at[number], out_sems.at[number]).wait()


def front(traces, kept_bins, window_starts, position):
    vmem = pl.BlockSpec(memory_space=pltpu.VMEM)
    smem = pl.BlockSpec(memory_space=pltpu.SMEM)
    hbm = pl.BlockSpec(memory_space=pltpu.HBM)
    given = [window_starts, kept_bins.reshape(1, K), traces]
    given = [pltpu.with_memory_space_constraint(array, pltpu.HBM) for array in given]
    return pl.pallas_call(
        front_kernel,
        out_shape=(pltpu.HBM((2, NF, KL, 2, WD, CB), jnp.bfloat16),)
        + (jax.ShapeDtypeStruct((NZ, HB, 2, WD, CB), jnp.bfloat16),) * NX,
        in_specs=[smem, hbm, hbm, hbm],
        out_specs=(hbm,) + (vmem,) * NX,
        scratch_shapes=[
            pltpu.SMEM((WD,), jnp.int32),
            pltpu.VMEM((1, K), jnp.int32),
            pltpu.VMEM((SEG, CB), jnp.bfloat16),
            pltpu.VMEM((SEG + 2 * WD, CB), jnp.float32),
            pltpu.VMEM((L, CB), jnp.float32),
            pltpu.VMEM((2 * K, L), jnp.bfloat16),
            pltpu.VMEM((2, L, 2 * CB), jnp.bfloat16),
            pltpu.VMEM((WD, 2 * K, CB), jnp.float32),
            pltpu.VMEM((NF, KL, 2, WD, CB), jnp.bfloat16),
            pltpu.SemaphoreType.DMA((3,)),
            pltpu.SemaphoreType.DMA((2,)),
        ],
        compiler_params=pltpu.CompilerParams(vmem_limit_bytes=40 * MIB),
        name="white",
    )(position, *given)


def left_side(refs):
    return jnp.concatenate([part_of(refs, 0), part_of(refs, 1)], axis=0)


def part_of(refs, e):
    parts = [ref[..., e, :, :].reshape(-1, CB) for ref in refs]
    return parts[0] if len(parts) == 1 else jnp.concatenate(parts, axis=0)


def right_side(refs):
    real, imag = part_of(refs, 0), part_of(refs, 1)
    return jnp.concatenate([jnp.concatenate([real, imag], axis=0), jnp.concatenate([-imag, real], axis=0)], axis=1)


def cross(left, right):
    found = lax.dot_general(left, right, (((0,), (0,)), ((), ())), preferred_element_type=jnp.float32)
    return (found * SCALE).astype(jnp.bfloat16)


def rounds_kernel(position, own, far, own_swapped, far_swapped, out):
    left = left_side([own])
    for r, ref in enumerate((own_swapped, far, far_swapped)):
        found = cross(left, right_side([ref]))
        for e in range(2):
            out[r, e, 0] = found[:, e * CB : (e + 1) * CB]


def rounds(position, both, both_swapped):
    own = pl.BlockSpec((1, NF, 1, 2, WD, CB), lambda k, position: (position[2], 0, k, 0, 0, 0))
    far = pl.BlockSpec((1, NF, 1, 2, WD, CB), lambda k, position: (1 - position[2], 0, k, 0, 0, 0))
    return pl.pallas_call(
        rounds_kernel,
        out_shape=jax.ShapeDtypeStruct((ROUNDS, 2, KL, CB, CB), jnp.bfloat16),
        grid_spec=pltpu.PrefetchScalarGridSpec(
            num_scalar_prefetch=1,
            grid=(KL,),
            in_specs=[own, far, own, far],
            out_specs=pl.BlockSpec((3, 2, 1, CB, CB), lambda k, position: (0, 0, k ^ (position[0] * HB), 0, 0)),
        ),
        compiler_params=pltpu.CompilerParams(vmem_limit_bytes=40 * MIB),
        name="rounds",
    )(position, both, both, both_swapped, both_swapped)


def between_kernel(position, both, *refs):
    sides, (to_far, to_side) = refs[:NZ], refs[NZ:]
    for k in range(HB):
        far = [both.at[1 - position[2], g ^ position[1], k] for g in range(NF)]
        side = [ref.at[:, k] for ref in sides]
        left, right = (jnp.concatenate([part_of(refs, 0), part_of(refs, 1)], axis=1) for refs in (far, side))
        found = lax.dot_general(left, right, (((0,), (0,)), ((), ())), preferred_element_type=jnp.float32)
        real = (found[:CB, :CB] + found[CB:, CB:]) * SCALE
        imag = (found[CB:, :CB] - found[:CB, CB:]) * SCALE
        to_far[0, k], to_far[1, k] = real.astype(jnp.bfloat16), imag.astype(jnp.bfloat16)
        to_side[0, k], to_side[1, k] = real.T.astype(jnp.bfloat16), (-imag).T.astype(jnp.bfloat16)


def between(position, both, side):
    vmem = pl.BlockSpec(memory_space=pltpu.VMEM)
    shape = jax.ShapeDtypeStruct((2, HB, CB, CB), jnp.bfloat16)
    return pl.pallas_call(
        between_kernel,
        out_shape=(shape, shape),
        in_specs=[pl.BlockSpec(memory_space=pltpu.SMEM)] + [vmem] * (1 + NZ),
        out_specs=(vmem, vmem),
        compiler_params=pltpu.CompilerParams(vmem_limit_bytes=40 * MIB),
        name="between",
    )(position, both, *side)


def place_kernel(position, first, second, base, out):
    @pl.when(pl.program_id(0) == 0)
    def _():
        out[0] = first[...]

    @pl.when(pl.program_id(0) == 1)
    def _():
        out[0] = second[...]


def place(position, first, second, base):
    whole = pl.BlockSpec((2, HB, CB, CB), lambda step, half: (0, 0, 0, 0))
    return pl.pallas_call(
        place_kernel,
        out_shape=jax.ShapeDtypeStruct(base.shape, base.dtype),
        grid_spec=pltpu.PrefetchScalarGridSpec(
            num_scalar_prefetch=1,
            grid=(2,),
            in_specs=[whole, whole, pl.BlockSpec(memory_space=pl.ANY)],
            out_specs=pl.BlockSpec((1, 2, HB, CB, CB), lambda step, position: (3, 0, position[0] ^ step, 0, 0)),
        ),
        input_output_aliases={3: 0},
        compiler_params=pltpu.CompilerParams(vmem_limit_bytes=40 * MIB),
        name="place",
    )(position, first, second, base)


def partner(block, mask):
    count = lax.axis_size("chan")
    return lax.ppermute(block, "chan", [(i, i ^ mask) for i in range(count)])


def send(block, chan_mask, freq_mask):
    moves = []
    for c in range(lax.axis_size("chan")):
        for f in range(NF):
            moves.append((c * NF + f, (c ^ chan_mask) * NF + (f ^ freq_mask)))
    return lax.ppermute(block, ("chan", "freq"), moves)


def together(*arrays):
    return lax.optimization_barrier(arrays)


def pair_groups(mask):
    pairs = [(c, c ^ mask) for c in range(lax.axis_size("chan")) if c < c ^ mask]
    return [[c * NF + f for c in pair for f in range(NF)] for pair in pairs]


def per_device(traces, kept_bins, window_starts):
    chan, freq = lax.axis_index("chan"), lax.axis_index("freq")
    position = jnp.stack([(chan >> 2) & 1, freq, (chan >> 1) & 1]).astype(jnp.int32)
    white, *crossed = front(traces, kept_bins, window_starts, position)
    crossed = [crossed[0]] + [send(crossed[e], 0, e) for e in range(1, NX)]
    crossed = [jnp.stack([piece[d] for piece in crossed]) for d in range(NZ)]
    side = [send(crossed[d], 6, d * NX) for d in range(NZ)]
    both = lax.all_to_all(
        white.reshape((2 * NF,) + white.shape[2:]),
        ("chan", "freq"),
        split_axis=0,
        concat_axis=0,
        tiled=True,
        axis_index_groups=pair_groups(2),
    ).reshape(white.shape)
    both, *side = together(both, *side)
    to_far, to_side = between(position, both, side)
    first, second = partner(to_far, 2), partner(to_side, 6)
    base = rounds(position, both, partner(both, 1))
    return place(position, first, second, base)


def solution(mesh):
    return jax.shard_map(
        per_device,
        mesh=mesh,
        in_specs=(P("freq", "chan"), P(), P("freq")),
        out_specs=P(None, None, "freq", "chan", None),
        check_vma=False,
    )
```
